32 devices in a mesh: tr: 8 (over z, x), tc: 4 (over y, core).
Axes of the slice: x: 2, y: 2, z: 4, core: 2. Of those that a mesh axis runs over, the one named last changes fastest.
Arguments:
- design: float32 [1024, 16384], P('tr', 'tc'), may hold values from -0.1875 to 0.1875
- taps: float32 [128], replicated, may hold values from -0.5 to 0.5
- order: int32 [16384], replicated, may hold values from 0 to 16383, each once
- normal_in: float32 [16384, 16384], P('tr', 'tc'), may hold values from -6 to 6
Outputs:
- normal_out: float32 [16384, 16384], P('tr', 'tc')
The draws below stay inside these ranges and needn't reach their ends.
Inputs may be any that keep to these rules, and one draw needn't show every extreme that they name: order is a permutation: every design column appears exactly once.
All inputs are finite; a program needn't handle non-finite values.
Results may differ from the reference program's by a relative error of at most 0.00005.
Values sent between devices are 32-bit elements; how exact they have to be, the bound alone decides.
A program may use at most 192 MiB of HBM per device.

```python
import jax
import jax.numpy as jnp
from jax import lax

C = 16384
TAPS = 128
ROW_DEV = 128
ROWS = 1024
N_TR = 8


def level_of(key, extent, split, smallest, high):
    loudness = 1.0
    for dim, blocks in split:
        draws = jax.random.uniform(jax.random.fold_in(jax.random.fold_in(key, 6), dim), (blocks,), jnp.float32, smallest / len(split), high / len(split))
        loudness = loudness * jnp.repeat(jnp.exp(draws), extent[dim] // blocks).reshape((-1,) + (1,) * (len(extent) - 1 - dim))
    return loudness


def gaussian(own_key, extent, width, most, split=(), dtype=jnp.bfloat16):
    level = level_of(own_key, extent, split, -0.22, 0.18) if split else 1.0
    array = jax.random.normal(own_key, extent, jnp.float32) * width * level
    return jnp.minimum(jnp.maximum(array, -most), most).astype(dtype)


def setup_inputs(seed: int = 0) -> dict:
    arg_keys = jax.random.split(jax.random.key(seed), 5)
    return {
        "design": gaussian(arg_keys[0], (ROWS, C), (1.0 / (ROW_DEV * N_TR) ** 0.5), 0.1875, ((0, 8), (1, 4)), jnp.float32),
        "taps": gaussian(arg_keys[1], (TAPS,), TAPS ** -0.5, 0.5, (), jnp.float32),
        "order": jax.random.permutation(arg_keys[2], C).astype(jnp.int32),
        "normal_in": gaussian(arg_keys[3], (C, C), 1.0, 6.0, ((0, 8), (1, 4)), jnp.float32),
    }


def reference(design, taps, order, normal_in):
    row_total = design.shape[0]
    padded = jnp.pad(design, ((TAPS - 1, 0), (0, 0)))

    def add_lag(lag_step, acc):
        start = (TAPS - 1 - lag_step)
        piece = lax.dynamic_slice_in_dim(padded, jnp.asarray(start).astype(jnp.int32), row_total, 0)
        return acc + taps[lag_step] * piece

    filtered = lax.fori_loop(0, TAPS, add_lag, jnp.zeros(design.shape, jnp.float32))
    ordered = jnp.take(filtered, order, axis=1)
    gram = lax.dot_general(ordered, ordered, (((0,), (0,)), ((), ())), precision=lax.Precision.HIGHEST, preferred_element_type=jnp.float32)
    return normal_in + jnp.tril(gram)
```

```python
import functools

import jax
import jax.numpy as jnp
from jax import lax
from jax.experimental import pallas as pl
from jax.experimental.pallas import tpu as pltpu
from jax.sharding import PartitionSpec as P

MESH = pl.DeviceIdType.MESH
VMEM_LIMIT = 56 * 1024 * 1024


def tile_of(extent, most):
    while extent % most:
        most //= 2
    return most


def toeplitz_of(taps, rows):
    count = taps.shape[0]
    line = jnp.concatenate([jnp.zeros((rows,), taps.dtype), taps, jnp.zeros((2 * rows + 1 - count,), taps.dtype)])
    length = line.shape[0]
    skewed = jnp.tile(line, 2 * rows)[: 2 * rows * (length - 1)].reshape(2 * rows, length - 1)
    return skewed[:, 2 * rows : 3 * rows]


def split(value):
    high = value.astype(jnp.bfloat16)
    return high, (value - high.astype(jnp.float32)).astype(jnp.bfloat16)


def permute_kernel(order_ref, src_ref, out_ref):
    count = out_ref.shape[0]
    unroll = 16

    def step(block, carry):
        base = pl.multiple_of(block * unroll, unroll)
        for lane in range(unroll):
            out_ref[pl.ds(base + lane, 1), :] = src_ref[pl.ds(order_ref[base + lane], 1), :]
        return carry

    lax.fori_loop(0, count // unroll, step, 0)


def permute_rows(source, order):
    count, width = order.shape[0], source.shape[1]
    return pl.pallas_call(
        permute_kernel,
        grid_spec=pltpu.PrefetchScalarGridSpec(
            num_scalar_prefetch=1,
            grid=(1,),
            in_specs=[pl.BlockSpec(source.shape, lambda i, o: (0, 0))],
            out_specs=pl.BlockSpec((count, width), lambda i, o: (0, 0)),
        ),
        out_shape=jax.ShapeDtypeStruct((count, width), jnp.float32),
        compiler_params=pltpu.CompilerParams(vmem_limit_bytes=VMEM_LIMIT),
    )(order, source)


def ring_next(index, count):
    even = lax.rem(index, 2) == 0
    up = jnp.where(index + 2 < count, index + 2, index + 1)
    down = jnp.where(index >= 2, index - 2, 0)
    return jnp.where(even, up, down)


def ring_place(index, count):
    half = lax.div(index, 2)
    return jnp.where(lax.rem(index, 2) == 0, half, count - 1 - half)


def ring_member(place, count):
    place = lax.rem(place + 2 * count, count)
    return jnp.where(place < count // 2, 2 * place, 2 * (count - 1 - place) + 1)


def spread_kernel(count, lanes, wide, tall, piece_ref, out_ref, own_sem, rs_sem, rr_sem, ls_sem, lr_sem, cs_sem, cr_sem, fill_sem):
    row = lax.axis_index("tr")
    col = lax.axis_index("tc")
    place = ring_place(row, count)
    right = ring_member(place + 1, count)
    left = ring_member(place - 1, count)
    owner = lax.div(row * tall, wide)
    offset = pl.multiple_of(lax.rem(row * tall, wide), tall)

    barrier = pltpu.get_barrier_semaphore()
    for near in (left, right):
        pl.semaphore_signal(barrier, inc=1, device_id=(near, col), device_id_type=MESH)

    @pl.when(col > 0)
    def _():
        pl.semaphore_signal(barrier, inc=1, device_id=(row, col - 1), device_id_type=MESH)

    @pl.when(col < lanes - 1)
    def _():
        pl.semaphore_signal(barrier, inc=1, device_id=(row, col + 1), device_id_type=MESH)

    peers = 2 + (col > 0).astype(jnp.int32) + (col < lanes - 1).astype(jnp.int32)
    pl.semaphore_wait(barrier, peers)

    own = pltpu.make_async_copy(piece_ref, out_ref.at[row, pl.ds(0, wide)], own_sem)
    own.start()

    steps = count // 2

    def ring(step, sign):
        slot = ring_member(place - sign * step, count)
        last = step == steps - 1
        begin, size = (0, wide)
        if last:
            begin, size = (0 if sign > 0 else wide // 2, wide // 2)
        rows = pl.ds(begin, size)
        source = piece_ref.at[rows] if step == 0 else out_ref.at[slot, rows]
        send, recv = (rs_sem, rr_sem) if sign > 0 else (ls_sem, lr_sem)
        return pltpu.make_async_remote_copy(
            src_ref=source,
            dst_ref=out_ref.at[slot, rows],
            send_sem=send.at[step],
            recv_sem=recv.at[step],
            device_id=(right if sign > 0 else left, col),
            device_id_type=MESH,
        )

    def chain(turn, slot, from_piece):
        if from_piece:
            source = piece_ref.at[pl.ds(offset, tall)]
        else:
            source = out_ref.at[slot, pl.ds(offset, tall)]
        target = out_ref.at[slot, pl.ds(wide, tall)]
        first = pltpu.make_async_remote_copy(
            src_ref=source, dst_ref=target, send_sem=cs_sem.at[turn], recv_sem=cr_sem.at[turn],
            device_id=(row, col - 1), device_id_type=MESH,
        )
        relay = pltpu.make_async_remote_copy(
            src_ref=target, dst_ref=target, send_sem=cs_sem.at[turn], recv_sem=cr_sem.at[turn],
            device_id=(row, col - 1), device_id_type=MESH,
        )
        fill = pltpu.make_async_copy(source, target, fill_sem.at[turn])
        return first, relay, fill

    offsets = [[0]] + [[-s, s] for s in range(1, steps)] + [[steps]]
    turns = []
    for group in offsets:
        turns.append([(len(sum(turns, [])) + i, off) for i, off in enumerate(group)])

    def chain_owner(level):
        for turn, off in turns[level]:
            first, _, fill = chain(turn, ring_member(place + off, count), level == 0)

            @pl.when(col == owner)
            def _():
                fill.start()

            @pl.when((col == owner) & (col > 0))
            def _():
                first.start()

    def chain_relay(level):
        for turn, off in turns[level]:
            _, relay, _ = chain(turn, ring_member(place + off, count), level == 0)

            @pl.when(col < owner)
            def _():
                relay.wait_recv()

            @pl.when((col < owner) & (col > 0))
            def _():
                relay.start()

    for step in range(steps):
        ring(step, 1).start()
        ring(step, -1).start()
        chain_owner(step)
        if step >= 1:
            chain_relay(step - 1)
        ring(step, 1).wait_recv()
        ring(step, -1).wait_recv()
    chain_owner(steps)
    chain_relay(steps - 1)
    chain_relay(steps)

    own.wait()
    for step in range(steps):
        ring(step, 1).wait_send()
        ring(step, -1).wait_send()
    for level in range(steps + 1):
        for turn, off in turns[level]:
            first, _, fill = chain(turn, ring_member(place + off, count), level == 0)

            @pl.when(col == owner)
            def _():
                fill.wait()

            @pl.when((col <= owner) & (col > 0))
            def _():
                first.wait_send()


def spread(piece, count, lanes, wide, tall):
    depth = piece.shape[1]
    steps = count // 2
    dma = pltpu.SemaphoreType.DMA
    return pl.pallas_call(
        functools.partial(spread_kernel, count, lanes, wide, tall),
        out_shape=jax.ShapeDtypeStruct((count, wide + tall, depth), jnp.float32),
        in_specs=[pl.BlockSpec(memory_space=pl.ANY)],
        out_specs=pl.BlockSpec(memory_space=pl.ANY),
        scratch_shapes=[
            dma, dma((steps,)), dma((steps,)), dma((steps,)), dma((steps,)), dma((count,)), dma((count,)), dma((count,)),
        ],
        compiler_params=pltpu.CompilerParams(collective_id=0, has_side_effects=True),
    )(piece)


def filter_kernel(data_ref, weight_ref, high_ref, low_ref):
    count, _, depth = data_ref.shape
    weight_high, weight_low = split(weight_ref[...])

    def product(left, right):
        return jnp.dot(left, right, preferred_element_type=jnp.float32)

    before = None
    for group in range(count):
        now = split(data_ref[group])
        if before is None:
            ext_high, ext_low = now
            use_high, use_low = weight_high[depth:], weight_low[depth:]
        else:
            ext_high = jnp.concatenate([before[0], now[0]], axis=1)
            ext_low = jnp.concatenate([before[1], now[1]], axis=1)
            use_high, use_low = weight_high, weight_low
        value = product(ext_high, use_high) + (product(ext_high, use_low) + product(ext_low, use_high))
        high, low = split(value)
        high_ref[:, group * depth : (group + 1) * depth] = high
        low_ref[:, group * depth : (group + 1) * depth] = low
        before = now


def filter_all(data, weight):
    count, total, depth = data.shape
    tile = tile_of(total, 512)
    out = jax.ShapeDtypeStruct((total, count * depth), jnp.bfloat16)
    spec = pl.BlockSpec((tile, count * depth), lambda i: (i, 0))
    return pl.pallas_call(
        filter_kernel,
        grid=(total // tile,),
        in_specs=[
            pl.BlockSpec((count, tile, depth), lambda i: (0, i, 0)),
            pl.BlockSpec(weight.shape, lambda i: (0, 0)),
        ],
        out_specs=[spec, spec],
        out_shape=[out, out],
        compiler_params=pltpu.CompilerParams(vmem_limit_bytes=VMEM_LIMIT),
    )(data, weight)


def gram_kernel(start_ref, ah_ref, al_ref, bh_ref, bl_ref, normal_ref, out_ref):
    tall, wide = out_ref.shape
    row = start_ref[0] + pl.program_id(0) * tall
    col = start_ref[1] + pl.program_id(1) * wide
    some = row + tall - 1 >= col
    full = row >= col + wide - 1

    def gram():
        def product(left, right):
            return lax.dot_general(left, right, (((1,), (1,)), ((), ())), preferred_element_type=jnp.float32)

        high = ah_ref[...]
        return product(high, bh_ref[...]) + (product(high, bl_ref[...]) + product(al_ref[...], bh_ref[...]))

    @pl.when(full)
    def _():
        out_ref[...] = normal_ref[...] + gram()

    @pl.when(some & jnp.logical_not(full))
    def _():
        rows = row + lax.broadcasted_iota(jnp.int32, (tall, wide), 0)
        cols = col + lax.broadcasted_iota(jnp.int32, (tall, wide), 1)
        out_ref[...] = normal_ref[...] + jnp.where(rows >= cols, gram(), 0.0)

    @pl.when(jnp.logical_not(some))
    def _():
        out_ref[...] = normal_ref[...]


def gram_add(start, high, low, normal_in, wide_total):
    tall_total = normal_in.shape[0]
    deep = high.shape[1]
    tall, wide = tile_of(tall_total, 1024), tile_of(wide_total, 512)
    skip = wide_total // tall
    left = pl.BlockSpec((tall, deep), lambda i, j, s: (skip + i, 0))
    right = pl.BlockSpec((wide, deep), lambda i, j, s: (j, 0))
    tile = pl.BlockSpec((tall, wide), lambda i, j, s: (i, j))
    return pl.pallas_call(
        gram_kernel,
        grid_spec=pltpu.PrefetchScalarGridSpec(
            num_scalar_prefetch=1,
            grid=(tall_total // tall, wide_total // wide),
            in_specs=[left, left, right, right, tile],
            out_specs=tile,
        ),
        out_shape=jax.ShapeDtypeStruct(normal_in.shape, jnp.float32),
        compiler_params=pltpu.CompilerParams(vmem_limit_bytes=VMEM_LIMIT),
    )(start, high, low, high, low, normal_in)


def body(design, taps, order, normal_in):
    depth = design.shape[0]
    count, lanes = lax.axis_size("tr"), lax.axis_size("tc")
    tall, wide = normal_in.shape
    row, col = lax.axis_index("tr"), lax.axis_index("tc")
    everything = lax.all_gather(design.T, "tc", axis=0, tiled=True)
    piece = permute_rows(everything, lax.dynamic_slice_in_dim(order, col * wide, wide, 0))
    data = spread(piece, count, lanes, wide, tall)
    high, low = filter_all(data, toeplitz_of(taps, depth))
    start = jnp.stack([row * tall, col * wide]).astype(jnp.int32)
    return gram_add(start, high, low, normal_in, wide)


def solution(mesh):
    return jax.shard_map(
        body,
        mesh=mesh,
        in_specs=(P("tr", "tc"), P(), P(), P("tr", "tc")),
        out_specs=P("tr", "tc"),
        check_vma=False,
    )
```

```python
import functools

import jax
import jax.numpy as jnp
from jax import lax
from jax.experimental import pallas as pl
from jax.experimental.pallas import tpu as pltpu
from jax.sharding import PartitionSpec as P

MESH = pl.DeviceIdType.MESH
VMEM_LIMIT = 56 * 1024 * 1024


def tile_of(extent, most):
    while extent % most:
        most //= 2
    return most


def toeplitz_of(taps, rows):
    count = taps.shape[0]
    line = jnp.concatenate([jnp.zeros((rows,), taps.dtype), taps, jnp.zeros((2 * rows + 1 - count,), taps.dtype)])
    length = line.shape[0]
    skewed = jnp.tile(line, 2 * rows)[: 2 * rows * (length - 1)].reshape(2 * rows, length - 1)
    return skewed[:, 2 * rows : 3 * rows]


def split(value):
    high = value.astype(jnp.bfloat16)
    return high, (value - high.astype(jnp.float32)).astype(jnp.bfloat16)


def permute_kernel(order_ref, src_ref, out_ref):
    count = out_ref.shape[0]
    unroll = 16

    def step(block, carry):
        base = pl.multiple_of(block * unroll, unroll)
        for lane in range(unroll):
            out_ref[pl.ds(base + lane, 1), :] = src_ref[pl.ds(order_ref[base + lane], 1), :]
        return carry

    lax.fori_loop(0, count // unroll, step, 0)


def permute_rows(source, order):
    count, width = order.shape[0], source.shape[1]
    return pl.pallas_call(
        permute_kernel,
        grid_spec=pltpu.PrefetchScalarGridSpec(
            num_scalar_prefetch=1,
            grid=(1,),
            in_specs=[pl.BlockSpec(source.shape, lambda i, o: (0, 0))],
            out_specs=pl.BlockSpec((count, width), lambda i, o: (0, 0)),
        ),
        out_shape=jax.ShapeDtypeStruct((count, width), jnp.float32),
        compiler_params=pltpu.CompilerParams(vmem_limit_bytes=VMEM_LIMIT),
    )(order, source)


def ring_next(index, count):
    even = lax.rem(index, 2) == 0
    up = jnp.where(index + 2 < count, index + 2, index + 1)
    down = jnp.where(index >= 2, index - 2, 0)
    return jnp.where(even, up, down)


def ring_place(index, count):
    half = lax.div(index, 2)
    return jnp.where(lax.rem(index, 2) == 0, half, count - 1 - half)


def ring_member(place, count):
    place = lax.rem(place + 2 * count, count)
    return jnp.where(place < count // 2, 2 * place, 2 * (count - 1 - place) + 1)


def spread_kernel(count, lanes, wide, tall, piece_ref, out_ref, own_sem, rs_sem, rr_sem, ls_sem, lr_sem, cs_sem, cr_sem):
    row = lax.axis_index("tr")
    col = lax.axis_index("tc")
    place = ring_place(row, count)
    right = ring_member(place + 1, count)
    left = ring_member(place - 1, count)
    owner = lax.div(row * tall, wide)
    offset = pl.multiple_of(lax.rem(row * tall, wide), tall)

    barrier = pltpu.get_barrier_semaphore()
    for near in (left, right):
        pl.semaphore_signal(barrier, inc=1, device_id=(near, col), device_id_type=MESH)

    @pl.when(col > 0)
    def _():
        pl.semaphore_signal(barrier, inc=1, device_id=(row, col - 1), device_id_type=MESH)

    @pl.when(col < lanes - 1)
    def _():
        pl.semaphore_signal(barrier, inc=1, device_id=(row, col + 1), device_id_type=MESH)

    peers = 2 + (col > 0).astype(jnp.int32) + (col < lanes - 1).astype(jnp.int32)
    pl.semaphore_wait(barrier, peers)

    own = pltpu.make_async_copy(piece_ref, out_ref.at[row, pl.ds(0, wide)], own_sem)
    own.start()

    steps = count // 2

    def ring(step, sign):
        slot = ring_member(place - sign * step, count)
        last = step == steps - 1
        begin, size = (0, wide)
        if last:
            begin, size = (0 if sign > 0 else wide // 2, wide // 2)
        rows = pl.ds(begin, size)
        source = piece_ref.at[rows] if step == 0 else out_ref.at[slot, rows]
        send, recv = (rs_sem, rr_sem) if sign > 0 else (ls_sem, lr_sem)
        return pltpu.make_async_remote_copy(
            src_ref=source,
            dst_ref=out_ref.at[slot, rows],
            send_sem=send.at[step],
            recv_sem=recv.at[step],
            device_id=(right if sign > 0 else left, col),
            device_id_type=MESH,
        )

    def chain(turn, slot, from_piece):
        if from_piece:
            source = piece_ref.at[pl.ds(offset, tall)]
        else:
            source = out_ref.at[slot, pl.ds(offset, tall)]
        target = out_ref.at[slot, pl.ds(wide, tall)]
        first = pltpu.make_async_remote_copy(
            src_ref=source, dst_ref=target, send_sem=cs_sem.at[turn], recv_sem=cr_sem.at[turn],
            device_id=(row, col - 1), device_id_type=MESH,
        )
        relay = pltpu.make_async_remote_copy(
            src_ref=target, dst_ref=target, send_sem=cs_sem.at[turn], recv_sem=cr_sem.at[turn],
            device_id=(row, col - 1), device_id_type=MESH,
        )
        return first, relay

    offsets = [[0]] + [[-s, s] for s in range(1, steps)] + [[steps]]
    turns = []
    for group in offsets:
        turns.append([(len(sum(turns, [])) + i, off) for i, off in enumerate(group)])

    def chain_owner(level):
        for turn, off in turns[level]:
            first, _ = chain(turn, ring_member(place + off, count), level == 0)

            @pl.when((col == owner) & (col > 0))
            def _():
                first.start()

    def chain_relay(level):
        for turn, off in turns[level]:
            _, relay = chain(turn, ring_member(place + off, count), level == 0)

            @pl.when(col < owner)
            def _():
                relay.wait_recv()

            @pl.when((col < owner) & (col > 0))
            def _():
                relay.start()

    for step in range(steps):
        ring(step, 1).start()
        ring(step, -1).start()
        chain_owner(step)
        chain_relay(step)
        ring(step, 1).wait_recv()
        ring(step, -1).wait_recv()
    chain_owner(steps)
    chain_relay(steps)

    own.wait()
    for step in range(steps):
        ring(step, 1).wait_send()
        ring(step, -1).wait_send()
    for level in range(steps + 1):
        for turn, off in turns[level]:
            first, _ = chain(turn, ring_member(place + off, count), level == 0)

            @pl.when((col <= owner) & (col > 0))
            def _():
                first.wait_send()


def spread(piece, count, lanes, wide, tall):
    depth = piece.shape[1]
    steps = count // 2
    dma = pltpu.SemaphoreType.DMA
    return pl.pallas_call(
        functools.partial(spread_kernel, count, lanes, wide, tall),
        out_shape=jax.ShapeDtypeStruct((count, wide + tall, depth), jnp.float32),
        in_specs=[pl.BlockSpec(memory_space=pl.ANY)],
        out_specs=pl.BlockSpec(memory_space=pl.ANY),
        scratch_shapes=[
            dma, dma((steps,)), dma((steps,)), dma((steps,)), dma((steps,)), dma((count,)), dma((count,)),
        ],
        compiler_params=pltpu.CompilerParams(collective_id=0, has_side_effects=True),
    )(piece)


def filter_kernel(data_ref, weight_ref, high_ref, low_ref):
    count, _, depth = data_ref.shape
    weight_high, weight_low = split(weight_ref[...])

    def product(left, right):
        return jnp.dot(left, right, preferred_element_type=jnp.float32)

    before = None
    for group in range(count):
        now = split(data_ref[group])
        if before is None:
            ext_high, ext_low = now
            use_high, use_low = weight_high[depth:], weight_low[depth:]
        else:
            ext_high = jnp.concatenate([before[0], now[0]], axis=1)
            ext_low = jnp.concatenate([before[1], now[1]], axis=1)
            use_high, use_low = weight_high, weight_low
        both = product(ext_high, jnp.concatenate([use_high, use_low], axis=1))
        value = both[:, :depth] + (both[:, depth:] + product(ext_low, use_high))
        high, low = split(value)
        high_ref[:, group * depth : (group + 1) * depth] = high
        low_ref[:, group * depth : (group + 1) * depth] = low
        before = now


def filter_all(data, weight):
    count, total, depth = data.shape
    tile = tile_of(total, 512)
    out = jax.ShapeDtypeStruct((total, count * depth), jnp.bfloat16)
    spec = pl.BlockSpec((tile, count * depth), lambda i: (i, 0))
    return pl.pallas_call(
        filter_kernel,
        grid=(total // tile,),
        in_specs=[
            pl.BlockSpec((count, tile, depth), lambda i: (0, i, 0)),
            pl.BlockSpec(weight.shape, lambda i: (0, 0)),
        ],
        out_specs=[spec, spec],
        out_shape=[out, out],
        compiler_params=pltpu.CompilerParams(vmem_limit_bytes=VMEM_LIMIT),
    )(data, weight)


def gram_kernel(start_ref, ah_ref, al_ref, bh_ref, bl_ref, normal_ref, out_ref):
    tall, wide = out_ref.shape
    row = start_ref[0] + pl.program_id(0) * tall
    col = start_ref[1] + pl.program_id(1) * wide
    some = row + tall - 1 >= col
    full = row >= col + wide - 1

    def gram():
        def product(left, right):
            return lax.dot_general(left, right, (((1,), (1,)), ((), ())), preferred_element_type=jnp.float32)

        high = ah_ref[...]
        return product(high, bh_ref[...]) + (product(high, bl_ref[...]) + product(al_ref[...], bh_ref[...]))

    @pl.when(full)
    def _():
        out_ref[...] = normal_ref[...] + gram()

    @pl.when(some & jnp.logical_not(full))
    def _():
        rows = row + lax.broadcasted_iota(jnp.int32, (tall, wide), 0)
        cols = col + lax.broadcasted_iota(jnp.int32, (tall, wide), 1)
        out_ref[...] = normal_ref[...] + jnp.where(rows >= cols, gram(), 0.0)

    @pl.when(jnp.logical_not(some))
    def _():
        out_ref[...] = normal_ref[...]


def gram_add(start, high, low, normal_in, wide_total):
    tall_total = normal_in.shape[0]
    deep = high.shape[1]
    tall, wide = tile_of(tall_total, 1024), tile_of(wide_total, 512)
    left = pl.BlockSpec((tall, deep), lambda i, j, s: (s[2] // tall + i, 0))
    right = pl.BlockSpec((wide, deep), lambda i, j, s: (j, 0))
    tile = pl.BlockSpec((tall, wide), lambda i, j, s: (i, j))
    return pl.pallas_call(
        gram_kernel,
        grid_spec=pltpu.PrefetchScalarGridSpec(
            num_scalar_prefetch=1,
            grid=(tall_total // tall, wide_total // wide),
            in_specs=[left, left, right, right, tile],
            out_specs=tile,
        ),
        out_shape=jax.ShapeDtypeStruct(normal_in.shape, jnp.float32),
        compiler_params=pltpu.CompilerParams(vmem_limit_bytes=VMEM_LIMIT),
    )(start, high, low, high, low, normal_in)


def body(design, taps, order, normal_in):
    depth = design.shape[0]
    count, lanes = lax.axis_size("tr"), lax.axis_size("tc")
    tall, wide = normal_in.shape
    row, col = lax.axis_index("tr"), lax.axis_index("tc")
    everything = lax.all_gather(design.T, "tc", axis=0, tiled=True)
    piece = permute_rows(everything, lax.dynamic_slice_in_dim(order, col * wide, wide, 0))
    data = spread(piece, count, lanes, wide, tall)
    high, low = filter_all(data, toeplitz_of(taps, depth))
    inside = jnp.where(lax.div(row * tall, wide) == col, lax.rem(row * tall, wide), wide)
    start = jnp.stack([row * tall, col * wide, inside]).astype(jnp.int32)
    return gram_add(start, high, low, normal_in, wide)


def solution(mesh):
    return jax.shard_map(
        body,
        mesh=mesh,
        in_specs=(P("tr", "tc"), P(), P(), P("tr", "tc")),
        out_specs=P("tr", "tc"),
        check_vma=False,
    )
```

```python
import functools

import jax
import jax.numpy as jnp
from jax import lax
from jax.experimental import pallas as pl
from jax.experimental.pallas import tpu as pltpu
from jax.sharding import PartitionSpec as P

MESH = pl.DeviceIdType.MESH
VMEM_LIMIT = 56 * 1024 * 1024


def tile_of(extent, most):
    while extent % most:
        most //= 2
    return most


def toeplitz_of(taps, rows):
    count = taps.shape[0]
    line = jnp.concatenate([jnp.zeros((rows,), taps.dtype), taps, jnp.zeros((2 * rows + 1 - count,), taps.dtype)])
    length = line.shape[0]
    skewed = jnp.tile(line, 2 * rows)[: 2 * rows * (length - 1)].reshape(2 * rows, length - 1)
    return skewed[:, 2 * rows : 3 * rows]


def split(value):
    high = value.astype(jnp.bfloat16)
    return high, (value - high.astype(jnp.float32)).astype(jnp.bfloat16)


def permute_kernel(order_ref, src_ref, out_ref):
    count = out_ref.shape[0]
    unroll = 16

    def step(block, carry):
        base = pl.multiple_of(block * unroll, unroll)
        for lane in range(unroll):
            out_ref[pl.ds(base + lane, 1), :] = src_ref[pl.ds(order_ref[base + lane], 1), :]
        return carry

    lax.fori_loop(0, count // unroll, step, 0)


def permute_rows(source, order):
    count, width = order.shape[0], source.shape[1]
    return pl.pallas_call(
        permute_kernel,
        grid_spec=pltpu.PrefetchScalarGridSpec(
            num_scalar_prefetch=1,
            grid=(1,),
            in_specs=[pl.BlockSpec(source.shape, lambda i, o: (0, 0))],
            out_specs=pl.BlockSpec((count, width), lambda i, o: (0, 0)),
        ),
        out_shape=jax.ShapeDtypeStruct((count, width), jnp.float32),
        compiler_params=pltpu.CompilerParams(vmem_limit_bytes=VMEM_LIMIT),
    )(order, source)


def ring_next(index, count):
    even = lax.rem(index, 2) == 0
    up = jnp.where(index + 2 < count, index + 2, index + 1)
    down = jnp.where(index >= 2, index - 2, 0)
    return jnp.where(even, up, down)


def ring_place(index, count):
    half = lax.div(index, 2)
    return jnp.where(lax.rem(index, 2) == 0, half, count - 1 - half)


def ring_member(place, count):
    place = lax.rem(place + 2 * count, count)
    return jnp.where(place < count // 2, 2 * place, 2 * (count - 1 - place) + 1)


def spread_kernel(
    count, lanes, wide, tall, piece_ref, weight_ref, high_ref, low_ref, out_ref, high_buf, low_buf,
    own_sem, rs_sem, rr_sem, ls_sem, lr_sem, cs_sem, cr_sem, high_sem, low_sem,
):
    row = lax.axis_index("tr")
    col = lax.axis_index("tc")
    place = ring_place(row, count)
    right = ring_member(place + 1, count)
    left = ring_member(place - 1, count)
    owner = lax.div(row * tall, wide)
    offset = pl.multiple_of(lax.rem(row * tall, wide), tall)

    barrier = pltpu.get_barrier_semaphore()
    for near in (left, right):
        pl.semaphore_signal(barrier, inc=1, device_id=(near, col), device_id_type=MESH)

    @pl.when(col > 0)
    def _():
        pl.semaphore_signal(barrier, inc=1, device_id=(row, col - 1), device_id_type=MESH)

    @pl.when(col < lanes - 1)
    def _():
        pl.semaphore_signal(barrier, inc=1, device_id=(row, col + 1), device_id_type=MESH)

    peers = 2 + (col > 0).astype(jnp.int32) + (col < lanes - 1).astype(jnp.int32)
    pl.semaphore_wait(barrier, peers)

    own = pltpu.make_async_copy(piece_ref, out_ref.at[row, pl.ds(0, wide)], own_sem)
    own.start()

    steps = count // 2

    def ring(step, sign):
        slot = ring_member(place - sign * step, count)
        last = step == steps - 1
        begin, size = (0, wide)
        if last:
            begin, size = (0 if sign > 0 else wide // 2, wide // 2)
        rows = pl.ds(begin, size)
        source = piece_ref.at[rows] if step == 0 else out_ref.at[slot, rows]
        send, recv = (rs_sem, rr_sem) if sign > 0 else (ls_sem, lr_sem)
        return pltpu.make_async_remote_copy(
            src_ref=source,
            dst_ref=out_ref.at[slot, rows],
            send_sem=send.at[step],
            recv_sem=recv.at[step],
            device_id=(right if sign > 0 else left, col),
            device_id_type=MESH,
        )

    def chain(turn, slot, from_piece):
        if from_piece:
            source = piece_ref.at[pl.ds(offset, tall)]
        else:
            source = out_ref.at[slot, pl.ds(offset, tall)]
        target = out_ref.at[slot, pl.ds(wide, tall)]
        first = pltpu.make_async_remote_copy(
            src_ref=source, dst_ref=target, send_sem=cs_sem.at[turn], recv_sem=cr_sem.at[turn],
            device_id=(row, col - 1), device_id_type=MESH,
        )
        relay = pltpu.make_async_remote_copy(
            src_ref=target, dst_ref=target, send_sem=cs_sem.at[turn], recv_sem=cr_sem.at[turn],
            device_id=(row, col - 1), device_id_type=MESH,
        )
        return first, relay

    offsets = [[0]] + [[-s, s] for s in range(1, steps)] + [[steps]]
    turns = []
    for group in offsets:
        turns.append([(len(sum(turns, [])) + i, off) for i, off in enumerate(group)])

    def chain_owner(level):
        for turn, off in turns[level]:
            first, _ = chain(turn, ring_member(place + off, count), level == 0)

            @pl.when((col == owner) & (col > 0))
            def _():
                first.start()

    def chain_relay(level):
        for turn, off in turns[level]:
            _, relay = chain(turn, ring_member(place + off, count), level == 0)

            @pl.when(col < owner)
            def _():
                relay.wait_recv()

            @pl.when((col < owner) & (col > 0))
            def _():
                relay.start()

    depth = piece_ref.shape[1]
    weight_high, weight_low = split(weight_ref[...])
    weight_both = jnp.concatenate([weight_high, weight_low], axis=1)

    def product(a, b):
        return jnp.dot(a, b, preferred_element_type=jnp.float32)

    def away(group):
        gap = lax.rem(ring_place(group, count) - place + count, count)
        return jnp.minimum(gap, count - gap)

    def ready(group):
        return jnp.maximum(away(group), away(jnp.maximum(group - 1, 0)))

    def flush(part, group, begin, size):
        rows = pl.ds(begin, size)
        lanes_of = pl.ds(pl.multiple_of(group * depth, depth), depth)
        return [
            pltpu.make_async_copy(buf.at[group, rows], ref.at[rows, lanes_of], sem.at[part, group])
            for buf, ref, sem in ((high_buf, high_ref, high_sem), (low_buf, low_ref, low_sem))
        ]

    def filter_part(level, part, begin, size):
        tile = tile_of(size, 256)

        def one(group, carry):
            @pl.when(ready(group) == level)
            def _():
                def rows_of(index, inner):
                    rows = pl.ds(pl.multiple_of(begin + index * tile, tile), tile)
                    old = jnp.where(group > 0, out_ref[jnp.maximum(group - 1, 0), rows, :], 0.0)
                    old_high, old_low = split(old)
                    new_high, new_low = split(out_ref[group, rows, :])
                    both = product(jnp.concatenate([old_high, new_high], axis=1), weight_both)
                    rest = product(jnp.concatenate([old_low, new_low], axis=1), weight_high)
                    high, low = split(both[:, :depth] + (both[:, depth:] + rest))
                    high_buf[group, rows, :] = high
                    low_buf[group, rows, :] = low
                    return inner

                lax.fori_loop(0, size // tile, rows_of, 0)
                for copy in flush(part, group, begin, size):
                    copy.start()

            return carry

        lax.fori_loop(0, count, one, 0)

    def work(level):
        chain_owner(level)
        filter_part(level, 0, 0, wide)
        chain_relay(level)

        @pl.when(col < owner)
        def _():
            filter_part(level, 1, wide, tall)

    for step in range(steps):
        ring(step, 1).start()
        ring(step, -1).start()
        if step == 0:
            own.wait()
        work(step)
        ring(step, 1).wait_recv()
        ring(step, -1).wait_recv()
    work(steps)

    for group in range(count):
        for copy in flush(0, group, 0, wide):
            copy.wait()

    @pl.when(col < owner)
    def _():
        for group in range(count):
            for copy in flush(1, group, wide, tall):
                copy.wait()

    for step in range(steps):
        ring(step, 1).wait_send()
        ring(step, -1).wait_send()
    for level in range(steps + 1):
        for turn, off in turns[level]:
            first, _ = chain(turn, ring_member(place + off, count), level == 0)

            @pl.when((col <= owner) & (col > 0))
            def _():
                first.wait_send()


def spread(piece, weight, count, lanes, wide, tall):
    depth = piece.shape[1]
    steps = count // 2
    dma = pltpu.SemaphoreType.DMA
    out = jax.ShapeDtypeStruct((wide + tall, count * depth), jnp.bfloat16)
    hold = (count, wide + tall, depth)
    return pl.pallas_call(
        functools.partial(spread_kernel, count, lanes, wide, tall),
        out_shape=[out, out],
        in_specs=[pl.BlockSpec(memory_space=pl.ANY), pl.BlockSpec(memory_space=pltpu.VMEM)],
        out_specs=[pl.BlockSpec(memory_space=pl.ANY)] * 2,
        scratch_shapes=[
            pltpu.VMEM(hold, jnp.float32), pltpu.VMEM(hold, jnp.bfloat16), pltpu.VMEM(hold, jnp.bfloat16),
            dma, dma((steps,)), dma((steps,)), dma((steps,)), dma((steps,)), dma((count,)), dma((count,)),
            dma((2, count)), dma((2, count)),
        ],
        compiler_params=pltpu.CompilerParams(
            collective_id=0, has_side_effects=True, vmem_limit_bytes=VMEM_LIMIT
        ),
    )(piece, weight)


def gram_kernel(start_ref, ah_ref, al_ref, bh_ref, bl_ref, normal_ref, out_ref):
    tall, wide = out_ref.shape
    row = start_ref[0] + pl.program_id(0) * tall
    col = start_ref[1] + pl.program_id(1) * wide
    some = row + tall - 1 >= col
    full = row >= col + wide - 1

    def gram():
        def product(left, right):
            return lax.dot_general(left, right, (((1,), (1,)), ((), ())), preferred_element_type=jnp.float32)

        high = ah_ref[...]
        return product(high, bh_ref[...]) + (product(high, bl_ref[...]) + product(al_ref[...], bh_ref[...]))

    @pl.when(full)
    def _():
        out_ref[...] = normal_ref[...] + gram()

    @pl.when(some & jnp.logical_not(full))
    def _():
        rows = row + lax.broadcasted_iota(jnp.int32, (tall, wide), 0)
        cols = col + lax.broadcasted_iota(jnp.int32, (tall, wide), 1)
        out_ref[...] = normal_ref[...] + jnp.where(rows >= cols, gram(), 0.0)

    @pl.when(jnp.logical_not(some))
    def _():
        out_ref[...] = normal_ref[...]


def gram_add(start, high, low, normal_in, wide_total):
    tall_total = normal_in.shape[0]
    deep = high.shape[1]
    tall, wide = tile_of(tall_total, 1024), tile_of(wide_total, 512)
    left = pl.BlockSpec((tall, deep), lambda i, j, s: (s[2] // tall + i, 0))
    right = pl.BlockSpec((wide, deep), lambda i, j, s: (j, 0))
    tile = pl.BlockSpec((tall, wide), lambda i, j, s: (i, j))
    return pl.pallas_call(
        gram_kernel,
        grid_spec=pltpu.PrefetchScalarGridSpec(
            num_scalar_prefetch=1,
            grid=(tall_total // tall, wide_total // wide),
            in_specs=[left, left, right, right, tile],
            out_specs=tile,
        ),
        out_shape=jax.ShapeDtypeStruct(normal_in.shape, jnp.float32),
        compiler_params=pltpu.CompilerParams(vmem_limit_bytes=VMEM_LIMIT),
    )(start, high, low, high, low, normal_in)


def body(design, taps, order, normal_in):
    depth = design.shape[0]
    count, lanes = lax.axis_size("tr"), lax.axis_size("tc")
    tall, wide = normal_in.shape
    row, col = lax.axis_index("tr"), lax.axis_index("tc")
    everything = lax.all_gather(design.T, "tc", axis=0, tiled=True)
    piece = permute_rows(everything, lax.dynamic_slice_in_dim(order, col * wide, wide, 0))
    high, low = spread(piece, toeplitz_of(taps, depth), count, lanes, wide, tall)
    inside = jnp.where(lax.div(row * tall, wide) == col, lax.rem(row * tall, wide), wide)
    start = jnp.stack([row * tall, col * wide, inside]).astype(jnp.int32)
    return gram_add(start, high, low, normal_in, wide)


def solution(mesh):
    return jax.shard_map(
        body,
        mesh=mesh,
        in_specs=(P("tr", "tc"), P(), P(), P("tr", "tc")),
        out_specs=P("tr", "tc"),
        check_vma=False,
    )
```
